32 devices in a mesh: gx: 4 (over y, x), gy: 8 (over z, core).
Axes of the slice: x: 2, y: 2, z: 4, core: 2. Of those that a mesh axis runs over, the one named last changes fastest.
Arguments:
- source: bfloat16 [288, 4, 8, 1024], P(None, 'gx', 'gy'), may hold values from -6 to 6
- slope: float32 [2, 144], replicated, may hold values from -6 to 6
- quad: bfloat16 [4, 4, 2, 20736], replicated, may hold values from -1 to 1, as said below
- pair: bfloat16 [2, 2, 2, 20736], replicated, may hold values from -1 to 1, as said below
Outputs:
- image: bfloat16 [288, 4, 8, 1024], P(None, 'gx', 'gy')
The draws below stay inside these ranges and needn't reach their ends.
Inputs may be any that keep to these rules, and one draw needn't show every extreme that they name: `quad`: translation coefficients. `pair`: translation coefficients.
All inputs are finite; a program needn't handle non-finite values.
Results may differ from the reference program's by a relative error of at most 0.02.
Values may be sent and summed in bfloat16 or wider, within the bound.
A program may use at most 64 MiB of HBM per device.

```python
import math
import jax
import jax.numpy as jnp

P_SIZE = 144
F = 288
SIDE = 32
BX = 128
BY = 256
N_GX = 4
N_GY = 8


def draw_noise(key, shape):
    return jnp.clip(jax.random.normal(key, shape, jnp.float32), -4.0, 4.0)


def draw_quad(key, part):
    target = jnp.arange(4)[:, None]
    child = jnp.arange(4)[None, :]
    differ = (target // 2 != child // 2).astype(jnp.int32) + (target % 2 != child % 2).astype(jnp.int32)
    real_core = jnp.where(differ == 0, 0.5, jnp.where(differ == 2, -0.5, 0.0))
    imag_core = jnp.where(differ == 1, 0.5, 0.0)
    core = jnp.stack([real_core, imag_core], -1).astype(jnp.float32)
    identity = jnp.eye(P_SIZE, dtype=jnp.float32)
    base = core[:, :, :, None, None] * identity
    noise = draw_noise(key, (4, 4, 2, P_SIZE, P_SIZE))
    return (base + 0.175 / math.sqrt(P_SIZE) * noise).reshape(4, 4, 2, P_SIZE * P_SIZE).astype(jnp.bfloat16)


def draw_pair(key, part):
    target = jnp.arange(2)[:, None]
    child = jnp.arange(2)[None, :]
    same = target == child
    real_core = jnp.where(same, 0.70710678, 0.0)
    imag_core = jnp.where(same, 0.0, 0.70710678)
    core = jnp.stack([real_core, imag_core], -1).astype(jnp.float32)
    identity = jnp.eye(P_SIZE, dtype=jnp.float32)
    base = core[:, :, :, None, None] * identity
    noise = draw_noise(key, (2, 2, 2, P_SIZE, P_SIZE))
    return (base + 0.247 / math.sqrt(P_SIZE) * noise).reshape(2, 2, 2, P_SIZE * P_SIZE).astype(jnp.bfloat16)


def block_scale(own_key, dims, pieces, smallest, largest):
    level = 1.0
    for dim, blocks in pieces:
        steps = jax.random.uniform(jax.random.fold_in(jax.random.fold_in(own_key, 6), dim), (blocks,), jnp.float32, smallest / len(pieces), largest / len(pieces))
        level = level * jnp.repeat(jnp.exp(steps), dims[dim] // blocks).reshape((-1,) + (1,) * (len(dims) - 1 - dim))
    return level


def scatter_about(own_key, dims, deviation, most, shards=(), held_as=jnp.bfloat16):
    drawn = deviation * jax.random.normal(own_key, dims, jnp.float32)
    if shards:
        drawn = drawn * block_scale(own_key, dims, shards, -0.22, 0.18)
    return jnp.clip(drawn, -most, most).astype(held_as)


def setup_inputs(seed: int = 0) -> dict:
    arg_keys = jax.random.split(jax.random.key(seed), 5)
    source = scatter_about(arg_keys[0], (F, N_GX, N_GY, SIDE * SIDE), 1.0, 6.0, ((1, 4), (2, 8)))
    slope = jnp.clip(jax.random.uniform(arg_keys[1], (2, P_SIZE), jnp.float32, -6.0, 6.0), -6.0, 6.0)
    quad = draw_quad(jax.random.fold_in(arg_keys[4], 71), 0)
    pair = draw_pair(jax.random.fold_in(arg_keys[4], 71), 0)
    return {"source": source, "slope": slope, "quad": quad, "pair": pair}


def complex_block(coefficients):
    real_part = coefficients[..., 0, :, :]
    imag_part = coefficients[..., 1, :, :]
    upper_rows = jnp.concatenate([real_part, -imag_part], -1)
    lower_rows = jnp.concatenate([imag_part, real_part], -1)
    return jnp.concatenate([upper_rows, lower_rows], -2)


def translate(current, depth, x_live, quad_block, pair_block):
    width_all, boxes_x, boxes_y = current.shape
    split_x = 2 if x_live else 1
    inner_x = (1 << depth) if x_live else 1
    inner_y = 1 << depth
    shape_seven = (width_all, boxes_x // (split_x * inner_x), split_x, inner_x, boxes_y // (2 * inner_y), 2, inner_y)
    shaped = current.reshape(shape_seven)
    stacked_rows = []
    for slot_x in range(split_x):
        columns = []
        for slot_y in range(2):
            summed = None
            for step_x in range(split_x):
                for step_y in range(2):
                    child_x = (slot_x + step_x) % 2
                    child_y = (slot_y + step_y) % 2
                    block_rows = shaped[:, :, child_x if x_live else 0, :, :, child_y, :]
                    if x_live:
                        matrix = quad_block[slot_x * 2 + slot_y, child_x * 2 + child_y]
                    else:
                        matrix = pair_block[slot_y, child_y]
                    product_term = jnp.dot(matrix.astype(jnp.float32), block_rows.reshape(width_all, -1).astype(jnp.float32), preferred_element_type=jnp.float32)
                    summed = product_term if summed is None else summed + product_term
            columns.append(summed.reshape(block_rows.shape))
        stacked_rows.append(jnp.stack(columns, 4))
    return jnp.stack(stacked_rows, 2).reshape(width_all, boxes_x, boxes_y)


def reference(source, slope, quad, pair):
    width_all = source.shape[0]
    half_width = width_all // 2
    tiles_x = source.shape[1]
    tiles_y = source.shape[2]
    grid = source.reshape(width_all, tiles_x, tiles_y, SIDE, SIDE).transpose(0, 1, 3, 2, 4).reshape(width_all, BX, BY)
    quad_block = complex_block(quad.reshape(4, 4, 2, P_SIZE, P_SIZE))
    pair_block = complex_block(pair.reshape(2, 2, 2, P_SIZE, P_SIZE))
    bits_x = BX.bit_length() - 1
    bits_y = BY.bit_length() - 1
    center_x = (jnp.arange(BX).astype(jnp.float32) + 0.5) / float(BX) - 0.5
    center_y = (jnp.arange(BY).astype(jnp.float32) + 0.5) / float(BY) - 0.5
    angle = slope[0][:, None, None] * center_x[None, :, None] + slope[1][:, None, None] * center_y[None, None, :]
    cosine_table = jnp.cos(angle)
    sine_table = jnp.sin(angle)
    current = grid
    for depth in range(max(bits_x, bits_y)):
        merged = translate(current, depth, depth < bits_x, quad_block, pair_block)
        real_part = merged[:half_width]
        imag_part = merged[half_width:]
        current = jnp.concatenate([real_part * cosine_table - imag_part * sine_table, real_part * sine_table + imag_part * cosine_table], 0).astype(jnp.bfloat16)
    return current.reshape(width_all, tiles_x, SIDE, tiles_y, SIDE).transpose(0, 1, 3, 2, 4).reshape(width_all, tiles_x, tiles_y, SIDE * SIDE)
```

```python
import functools
import jax
import jax.numpy as jnp
import numpy as np
from jax import lax
from jax.experimental import pallas as pl
from jax.experimental.pallas import tpu as pltpu
from jax.sharding import PartitionSpec as P

P_SIZE = 144
SIDE = 32


def partner(value, axis, stride):
    mask = 2**stride
    pairs = [(source, source ^ mask) for source in range(lax.axis_size(axis))]
    return lax.ppermute(value, axis, pairs)


def complex_block(coefficients):
    real_part = coefficients[..., 0, :, :]
    imag_part = coefficients[..., 1, :, :]
    upper_rows = jnp.concatenate([real_part, -imag_part], -1)
    lower_rows = jnp.concatenate([imag_part, real_part], -1)
    return jnp.concatenate([upper_rows, lower_rows], -2)


def translate(neighbours, mode_x, mode_y, depth, target_x, target_y, quad_block, pair_block):
    width_all, boxes_x, boxes_y = neighbours[0, 0].shape
    split_x = 2 if mode_x == "local" else 1
    inner_x = 1 << depth if mode_x == "local" else 1
    split_y = 2 if mode_y == "local" else 1
    inner_y = 1 << depth if mode_y == "local" else 1
    shape_seven = (
        width_all,
        boxes_x // (split_x * inner_x),
        split_x,
        inner_x,
        boxes_y // (split_y * inner_y),
        split_y,
        inner_y,
    )
    shaped = {}
    for source_key in neighbours:
        shaped[source_key] = neighbours[source_key].reshape(shape_seven)
    steps_x = [0, 1] if mode_x != "none" else [0]
    steps_y = [0, 1]
    stacked_rows = []
    for slot_x in range(split_x):
        columns = []
        for slot_y in range(split_y):
            chosen_x = slot_x if mode_x == "local" else target_x
            chosen_y = slot_y if mode_y == "local" else target_y
            summed = None
            for step_x in steps_x:
                for step_y in steps_y:
                    source_key = (
                        step_x if mode_x == "device" else 0,
                        step_y if mode_y == "device" else 0,
                    )
                    from_x = (slot_x + step_x) % 2 if mode_x == "local" else 0
                    from_y = (slot_y + step_y) % 2 if mode_y == "local" else 0
                    block_rows = shaped[source_key][:, :, from_x, :, :, from_y, :]
                    child_x = (chosen_x + step_x) % 2
                    child_y = (chosen_y + step_y) % 2
                    if mode_x == "none":
                        matrix = pair_block[chosen_y, child_y]
                    else:
                        matrix = quad_block[chosen_x * 2 + chosen_y, child_x * 2 + child_y]
                    product_term = jnp.dot(
                        matrix,
                        block_rows.reshape(width_all, -1),
                        preferred_element_type=jnp.float32,
                    )
                    summed = product_term if summed is None else summed + product_term
            columns.append(summed.reshape(block_rows.shape))
        stacked_rows.append(jnp.stack(columns, 4))
    return jnp.stack(stacked_rows, 2).reshape(width_all, boxes_x, boxes_y)


def rotate(merged, cosine_table, sine_table):
    half_width = merged.shape[0] // 2
    real_part = merged[:half_width]
    imag_part = merged[half_width:]
    return jnp.concatenate(
        [
            real_part * cosine_table - imag_part * sine_table,
            real_part * sine_table + imag_part * cosine_table,
        ],
        0,
    ).astype(jnp.bfloat16)


def local(source, slope, quad, pair):
    width_all = source.shape[0]
    boxes_x = SIDE
    boxes_y = SIDE
    count_x = lax.axis_size("gx")
    count_y = lax.axis_size("gy")
    local_bits_x = boxes_x.bit_length() - 1
    local_bits_y = boxes_y.bit_length() - 1
    device_bits_x = count_x.bit_length() - 1
    device_bits_y = count_y.bit_length() - 1
    levels_x = local_bits_x + device_bits_x
    levels_y = local_bits_y + device_bits_y
    place_x = lax.axis_index("gx")
    place_y = lax.axis_index("gy")
    quad_block = complex_block(quad.reshape(4, 4, 2, P_SIZE, P_SIZE))
    pair_block = complex_block(pair.reshape(2, 2, 2, P_SIZE, P_SIZE))
    center_x = ((place_x * boxes_x + jnp.arange(boxes_x)).astype(jnp.float32) + 0.5) / float(
        boxes_x * count_x
    ) - 0.5
    center_y = ((place_y * boxes_y + jnp.arange(boxes_y)).astype(jnp.float32) + 0.5) / float(
        boxes_y * count_y
    ) - 0.5
    angle = (
        slope[0][:, None, None] * center_x[None, :, None]
        + slope[1][:, None, None] * center_y[None, None, :]
    )
    cosine_table = jnp.cos(angle)
    sine_table = jnp.sin(angle)
    current = source.reshape(width_all, boxes_x, boxes_y)
    last_level = max(levels_x, levels_y)
    for depth in range(last_level):
        mode_x = "local" if depth < local_bits_x else "device" if depth < levels_x else "none"
        mode_y = "local" if depth < local_bits_y else "device"
        neighbours = {(0, 0): current}
        target_x = 0
        target_y = 0
        if mode_x == "device":
            shift_x = depth - local_bits_x
            shift_y = depth - local_bits_y
            target_x = place_x // (1 << shift_x) % 2
            target_y = place_y // (1 << shift_y) % 2
            across_x = partner(current, "gx", shift_x)
            paired = partner(jnp.stack([current, across_x]), "gy", shift_y)
            across_y = paired[0]
            across_both = paired[1]
            neighbours[1, 0] = across_x
            neighbours[0, 1] = across_y
            neighbours[1, 1] = across_both
        elif mode_y == "device":
            shift_y = depth - local_bits_y
            target_y = place_y // (1 << shift_y) % 2
            neighbours[0, 1] = partner(current, "gy", shift_y)
        merged = translate(
            neighbours, mode_x, mode_y, depth, target_x, target_y, quad_block, pair_block
        )
        current = rotate(merged, cosine_table, sine_table)
    return current.reshape(width_all, 1, 1, boxes_x * boxes_y)

LANES = 128
CHIPS = 16
BF16 = jnp.bfloat16
F32 = jnp.float32
MESH_ID = pl.DeviceIdType.MESH


def plan():
    slots = [("i", 4), ("i", 3), ("i", 2)]
    lanes = {64: ("i", 1), 32: ("i", 0)}
    for bit in range(5):
        lanes[1 << bit] = ("j", bit)
    steps = []
    for level in range(5):
        swaps = []
        need = [("i", level), ("j", level)]
        for bit in need:
            if bit in slots:
                continue
            stride = [s for s in lanes if lanes[s] == bit][0]
            free = [k for k in range(3) if slots[k] not in need]
            slot = free[0]
            swaps.append((slot, stride))
            slots[slot], lanes[stride] = lanes[stride], slots[slot]
        steps.append((swaps, slots.index(need[0]), slots.index(need[1])))
    return steps, slots, lanes


STEPS, END_SLOTS, END_LANES = plan()


def home_columns():
    columns = np.zeros(1024, np.int64)
    for place in range(1024):
        block, lane = place // LANES, place % LANES
        values = {END_SLOTS[k]: block >> (2 - k) & 1 for k in range(3)}
        for stride in END_LANES:
            values[END_LANES[stride]] = 1 if lane & stride else 0
        i = sum(values["i", b] << b for b in range(5))
        j = sum(values["j", b] << b for b in range(5))
        columns[place] = i * 32 + j
    return columns


def swap_pair(first, second, stride):
    mask = (lax.broadcasted_iota(jnp.int32, first.shape, 1) & stride) == 0
    low = jnp.where(mask, first, pltpu.roll(second, stride, 1))
    high = jnp.where(mask, pltpu.roll(first, LANES - stride, 1), second)
    return low, high


def slot_index(bits):
    return bits[0] * 4 + bits[1] * 2 + bits[2]


def turn(merged, cosine, sine):
    real_part, imag_part = merged[:P_SIZE], merged[P_SIZE:]
    return jnp.concatenate(
        [real_part * cosine - imag_part * sine, real_part * sine + imag_part * cosine], 0
    ).astype(BF16)


def near_kernel(source_ref, table_ref, weight_ref, out_ref, table_out, state):
    width = 2 * P_SIZE
    for block in range(8):
        columns = pl.ds(block * LANES, LANES)
        state[block, 0:width, :] = source_ref[:, columns]
        state[block, width : 2 * width, :] = table_ref[:, columns]
    for swaps, slot_x, slot_y in STEPS:
        for slot, stride in swaps:
            mask = 4 >> slot
            for block in range(8):
                if not block & mask:
                    low, high = swap_pair(state[block], state[block | mask], stride)
                    state[block] = low
                    state[block | mask] = high
        rest = 3 - slot_x - slot_y

        def at(tx, ty, g):
            bits = [0, 0, 0]
            bits[slot_x], bits[slot_y], bits[rest] = tx, ty, g
            return slot_index(bits)

        stacked = jnp.concatenate(
            [
                jnp.concatenate([state[at(c // 2, c % 2, g), 0:width, :] for g in range(2)], 1)
                for c in range(4)
            ],
            0,
        )
        for t in range(4):
            merged = jnp.dot(
                weight_ref[t * width : (t + 1) * width, :], stacked, preferred_element_type=F32
            )
            for g in range(2):
                block = at(t // 2, t % 2, g)
                table = state[block, width : 2 * width, :].astype(F32)
                state[block, 0:width, :] = turn(
                    merged[:, g * LANES : (g + 1) * LANES], table[:P_SIZE], table[P_SIZE:]
                )
    for block in range(8):
        low, high = swap_pair(
            state[block, 0:P_SIZE, :], state[block, P_SIZE:width, :], 64
        )
        out_ref[2 * block] = low
        out_ref[2 * block + 1] = high
        table_out[block] = state[block, width : 2 * width, :]


def far_kernel(own_ref, table_ref, shift_ref, weight_ref, pair_ref, out_ref, state, tables, other):
    width = 2 * P_SIZE
    half = lax.axis_index("gy") // 2 % 2
    chip = lax.axis_index("gx") * 4 + lax.axis_index("gy") // 2
    core = lax.axis_index("gy") % 2
    lane = lax.broadcasted_iota(jnp.int32, (P_SIZE, LANES), 1)
    keep = (lane // 64) == half
    table = table_ref[chip // 2].astype(F32)
    base = []
    for k in range(2):
        part = table[k * P_SIZE : (k + 1) * P_SIZE]
        base.append(jnp.where(keep, part, pltpu.roll(part, 64, 1)))

    def chip_of(y, x, z1, z0):
        return y * 8 + x * 4 + z1 * 2 + z0

    for y in range(2):
        for x in range(2):
            for z0 in range(2):
                block = y * 4 + x * 2 + z0
                pick = []
                for k in range(2):
                    low = shift_ref[k, :, chip_of(y, x, 0, z0) : chip_of(y, x, 0, z0) + 1]
                    high = shift_ref[k, :, chip_of(y, x, 1, z0) : chip_of(y, x, 1, z0) + 1]
                    pick.append(jnp.where(lane < 64, low, high))
                tables[block, 0] = base[0] * pick[0] - base[1] * pick[1]
                tables[block, 1] = base[0] * pick[1] + base[1] * pick[0]
                for step in range(2):
                    low, high = swap_pair(
                        own_ref[step, chip_of(y, x, 0, z0)], own_ref[step, chip_of(y, x, 1, z0)], 64
                    )
                    target = state if step == 0 else other
                    target[block, 0:P_SIZE, :] = low
                    target[block, P_SIZE:width, :] = high

    def emit(merged, blocks):
        for n, block in enumerate(blocks):
            state[block] = turn(
                merged[:, n * LANES : (n + 1) * LANES], tables[block, 0], tables[block, 1]
            )

    groups = [(y, z0) for y in range(2) for z0 in range(2)]
    stacked = jnp.concatenate(
        [
            jnp.concatenate([ref[y * 4 + x * 2 + z0] for y, z0 in groups], 1)
            for x in range(2)
            for ref in (state, other)
        ],
        0,
    )
    is_first = core == 0
    swapped = []
    for x in range(2):
        mine = stacked[(2 * x) * width : (2 * x + 1) * width]
        theirs = stacked[(2 * x + 1) * width : (2 * x + 2) * width]
        swapped += [jnp.where(is_first, mine, theirs), jnp.where(is_first, theirs, mine)]
    stacked = jnp.concatenate(swapped, 0)
    for x in range(2):
        row = pl.multiple_of((x * 2 + core) * width, width)
        merged = jnp.dot(
            weight_ref[pl.ds(row, width), :], stacked, preferred_element_type=F32
        )
        emit(merged, [y * 4 + x * 2 + z0 for y, z0 in groups])
    stacked = jnp.concatenate(
        [
            jnp.concatenate([state[c // 2 * 4 + x * 2 + c % 2] for x in range(2)], 1)
            for c in range(4)
        ],
        0,
    )
    for t in range(4):
        merged = jnp.dot(
            weight_ref[t * width : (t + 1) * width, :], stacked, preferred_element_type=F32
        )
        emit(merged, [t // 2 * 4 + x * 2 + t % 2 for x in range(2)])
    for block in range(4):
        low, high = swap_pair(state[block], state[block + 4], 64)
        state[block] = low
        state[block + 4] = high
        for k in range(2):
            low, high = swap_pair(tables[block, k], tables[block + 4, k], 64)
            tables[block, k] = low
            tables[block + 4, k] = high
    stacked = jnp.concatenate(
        [jnp.concatenate([state[c * 4 + g] for g in range(4)], 1) for c in range(2)], 0
    )
    for t in range(2):
        merged = jnp.dot(
            pair_ref[t * width : (t + 1) * width, :], stacked, preferred_element_type=F32
        )
        emit(merged, [t * 4 + g for g in range(4)])
    for z1 in range(2):
        for x in range(2):
            for z0 in range(2):
                block = z1 * 4 + x * 2 + z0
                low, high = swap_pair(
                    state[block, 0:P_SIZE, :], state[block, P_SIZE:width, :], 64
                )
                out_ref[chip_of(0, x, z1, z0)] = low
                out_ref[chip_of(1, x, z1, z0)] = high


def home_kernel(block_ref, order_ref, out_ref, state):
    for block in range(8):
        low, high = swap_pair(block_ref[2 * block], block_ref[2 * block + 1], 64)
        columns = slice(block * LANES, (block + 1) * LANES)
        state[0:P_SIZE, columns] = low
        state[P_SIZE : 2 * P_SIZE, columns] = high
    for part in range(4):
        columns = slice(part * 256, (part + 1) * 256)
        out_ref[:, columns] = jnp.dot(
            state[...], order_ref[:, columns], preferred_element_type=F32
        ).astype(BF16)


def trade_kernel(both, in_ref, out_ref, send_sem, recv_sem, pass_send, pass_recv, own_sem):
    gx = lax.axis_index("gx")
    gy = lax.axis_index("gy")
    core = gy % 2
    chip = gx * 4 + gy // 2
    mate = (gx, gy // 2 * 2 + (1 - core))

    def place(index):
        return (index // 4, index % 4 * 2 + core)

    barrier = pltpu.get_barrier_semaphore()
    for k in range(1, CHIPS):
        pl.semaphore_signal(
            barrier, inc=1, device_id=place((chip + k) % CHIPS), device_id_type=MESH_ID
        )
    if both:
        pl.semaphore_signal(barrier, inc=1, device_id=mate, device_id_type=MESH_ID)
    pl.semaphore_wait(barrier, CHIPS if both else CHIPS - 1)

    def landing(which, index):
        return out_ref.at[which, index] if both else out_ref.at[index]

    sends = []
    for k in range(1, CHIPS):
        dest = (chip + k) % CHIPS
        copy = pltpu.make_async_remote_copy(
            src_ref=in_ref.at[dest],
            dst_ref=landing(0, chip),
            send_sem=send_sem.at[k],
            recv_sem=recv_sem.at[k],
            device_id=place(dest),
            device_id_type=MESH_ID,
        )
        copy.start()
        sends.append(copy)
    own = pltpu.make_async_copy(in_ref.at[chip], landing(0, chip), own_sem)
    own.start()

    def forward(k, src):
        index = (chip + CHIPS - k) % CHIPS
        copy = pltpu.make_async_remote_copy(
            src_ref=src,
            dst_ref=landing(1, index),
            send_sem=pass_send.at[k],
            recv_sem=pass_recv.at[k],
            device_id=mate,
            device_id_type=MESH_ID,
        )
        copy.start()
        return copy

    passes = []
    if both:
        passes.append(forward(0, in_ref.at[chip]))
    for k in range(1, CHIPS):
        sends[k - 1].wait_recv()
        if both:
            passes.append(forward(k, landing(0, (chip + CHIPS - k) % CHIPS)))
    own.wait()
    for copy in sends:
        copy.wait_send()
    for copy in passes:
        copy.wait()


def trade(blocks, both, identity):
    shape = ((2,) if both else ()) + blocks.shape
    return pl.pallas_call(
        functools.partial(trade_kernel, both),
        out_shape=jax.ShapeDtypeStruct(shape, BF16),
        in_specs=[pl.BlockSpec(memory_space=pl.ANY)],
        out_specs=pl.BlockSpec(memory_space=pl.ANY),
        scratch_shapes=[pltpu.SemaphoreType.DMA((CHIPS,))] * 4 + [pltpu.SemaphoreType.DMA],
        compiler_params=pltpu.CompilerParams(collective_id=identity, has_side_effects=True),
    )(blocks)


def merged_block(coefficients, count):
    shaped = coefficients.reshape(count, count, 2, P_SIZE, P_SIZE)
    real_part = shaped[:, :, 0].transpose(0, 2, 1, 3)
    imag_part = shaped[:, :, 1].transpose(0, 2, 1, 3)
    upper = jnp.stack([real_part, -imag_part], 3)
    lower = jnp.stack([imag_part, real_part], 3)
    size = count * 2 * P_SIZE
    return jnp.stack([upper, lower], 1).reshape(size, size)


def turned(angle):
    return jnp.cos(angle), jnp.sin(angle)


def traded(source, slope, quad, pair):
    width_all = source.shape[0]
    count_x = lax.axis_size("gx")
    count_y = lax.axis_size("gy")
    place_x = lax.axis_index("gx")
    place_y = lax.axis_index("gy")
    core = place_y % 2
    total_x = float(SIDE * count_x)
    total_y = float(SIDE * count_y)
    steps = jnp.arange(SIDE)
    center_x = ((place_x * SIDE + steps).astype(F32) + 0.5) / total_x - 0.5
    center_y = ((place_y * SIDE + steps).astype(F32) + 0.5) / total_y - 0.5
    tiles = jnp.arange(CHIPS)
    far_x = ((tiles // 4 - place_x) * SIDE).astype(F32) / total_x
    far_y = ((tiles % 4 * 2 + core - place_y) * SIDE).astype(F32) / total_y
    angle = jnp.concatenate(
        [
            slope[0][:, None] * center_x[None],
            slope[1][:, None] * center_y[None],
            slope[0][:, None] * far_x[None] + slope[1][:, None] * far_y[None],
        ],
        1,
    )
    cosine, sine = turned(angle)
    cos_x, sin_x = cosine[:, :SIDE, None], sine[:, :SIDE, None]
    cos_y, sin_y = cosine[:, None, SIDE : 2 * SIDE], sine[:, None, SIDE : 2 * SIDE]
    table = jnp.concatenate([cos_x * cos_y - sin_x * sin_y, cos_x * sin_y + sin_x * cos_y], 0)
    table = table.astype(BF16).reshape(width_all, SIDE * SIDE)
    shift = jnp.stack([cosine[:, 2 * SIDE :], sine[:, 2 * SIDE :]])
    weight = merged_block(quad, 4)
    pair_weight = merged_block(pair, 2)
    order = jnp.asarray(home_columns()[:, None] == np.arange(SIDE * SIDE)[None], BF16)
    roomy = pltpu.CompilerParams(vmem_limit_bytes=50 * 1024 * 1024)
    block_shape = jax.ShapeDtypeStruct((CHIPS, P_SIZE, LANES), BF16)
    blocks, near_table = pl.pallas_call(
        near_kernel,
        out_shape=(block_shape, jax.ShapeDtypeStruct((8, width_all, LANES), BF16)),
        scratch_shapes=[pltpu.VMEM((8, 2 * width_all, LANES), BF16)],
        compiler_params=roomy,
    )(source.reshape(width_all, SIDE * SIDE), table, weight)
    gathered = trade(blocks, True, 0)
    results = pl.pallas_call(
        far_kernel,
        out_shape=block_shape,
        scratch_shapes=[
            pltpu.VMEM((8, width_all, LANES), BF16),
            pltpu.VMEM((8, 2, P_SIZE, LANES), F32),
            pltpu.VMEM((8, width_all, LANES), BF16),
        ],
        compiler_params=roomy,
    )(gathered, near_table, shift, weight, pair_weight)
    returned = trade(results, False, 1)
    image = pl.pallas_call(
        home_kernel,
        out_shape=jax.ShapeDtypeStruct((width_all, SIDE * SIDE), BF16),
        scratch_shapes=[pltpu.VMEM((width_all, SIDE * SIDE), BF16)],
        compiler_params=roomy,
    )(returned, order)
    return image.reshape(width_all, 1, 1, SIDE * SIDE)


def solution(mesh):
    in_specs = (P(None, "gx", "gy", None), P(), P(), P())
    out_specs = P(None, "gx", "gy", None)
    fits = mesh.shape["gx"] == 4 and mesh.shape["gy"] == 8
    body = traded if fits else local
    return jax.shard_map(body, mesh=mesh, in_specs=in_specs, out_specs=out_specs, check_vma=False)
```

```python
import functools
import jax
import jax.numpy as jnp
import numpy as np
from jax import lax
from jax.experimental import pallas as pl
from jax.experimental.pallas import tpu as pltpu
from jax.sharding import PartitionSpec as P

P_SIZE = 144
SIDE = 32


def partner(value, axis, stride):
    mask = 2**stride
    pairs = [(source, source ^ mask) for source in range(lax.axis_size(axis))]
    return lax.ppermute(value, axis, pairs)


def complex_block(coefficients):
    real_part = coefficients[..., 0, :, :]
    imag_part = coefficients[..., 1, :, :]
    upper_rows = jnp.concatenate([real_part, -imag_part], -1)
    lower_rows = jnp.concatenate([imag_part, real_part], -1)
    return jnp.concatenate([upper_rows, lower_rows], -2)


def translate(neighbours, mode_x, mode_y, depth, target_x, target_y, quad_block, pair_block):
    width_all, boxes_x, boxes_y = neighbours[0, 0].shape
    split_x = 2 if mode_x == "local" else 1
    inner_x = 1 << depth if mode_x == "local" else 1
    split_y = 2 if mode_y == "local" else 1
    inner_y = 1 << depth if mode_y == "local" else 1
    shape_seven = (
        width_all,
        boxes_x // (split_x * inner_x),
        split_x,
        inner_x,
        boxes_y // (split_y * inner_y),
        split_y,
        inner_y,
    )
    shaped = {}
    for source_key in neighbours:
        shaped[source_key] = neighbours[source_key].reshape(shape_seven)
    steps_x = [0, 1] if mode_x != "none" else [0]
    steps_y = [0, 1]
    stacked_rows = []
    for slot_x in range(split_x):
        columns = []
        for slot_y in range(split_y):
            chosen_x = slot_x if mode_x == "local" else target_x
            chosen_y = slot_y if mode_y == "local" else target_y
            summed = None
            for step_x in steps_x:
                for step_y in steps_y:
                    source_key = (
                        step_x if mode_x == "device" else 0,
                        step_y if mode_y == "device" else 0,
                    )
                    from_x = (slot_x + step_x) % 2 if mode_x == "local" else 0
                    from_y = (slot_y + step_y) % 2 if mode_y == "local" else 0
                    block_rows = shaped[source_key][:, :, from_x, :, :, from_y, :]
                    child_x = (chosen_x + step_x) % 2
                    child_y = (chosen_y + step_y) % 2
                    if mode_x == "none":
                        matrix = pair_block[chosen_y, child_y]
                    else:
                        matrix = quad_block[chosen_x * 2 + chosen_y, child_x * 2 + child_y]
                    product_term = jnp.dot(
                        matrix,
                        block_rows.reshape(width_all, -1),
                        preferred_element_type=jnp.float32,
                    )
                    summed = product_term if summed is None else summed + product_term
            columns.append(summed.reshape(block_rows.shape))
        stacked_rows.append(jnp.stack(columns, 4))
    return jnp.stack(stacked_rows, 2).reshape(width_all, boxes_x, boxes_y)


def rotate(merged, cosine_table, sine_table):
    half_width = merged.shape[0] // 2
    real_part = merged[:half_width]
    imag_part = merged[half_width:]
    return jnp.concatenate(
        [
            real_part * cosine_table - imag_part * sine_table,
            real_part * sine_table + imag_part * cosine_table,
        ],
        0,
    ).astype(jnp.bfloat16)


def local(source, slope, quad, pair):
    width_all = source.shape[0]
    boxes_x = SIDE
    boxes_y = SIDE
    count_x = lax.axis_size("gx")
    count_y = lax.axis_size("gy")
    local_bits_x = boxes_x.bit_length() - 1
    local_bits_y = boxes_y.bit_length() - 1
    device_bits_x = count_x.bit_length() - 1
    device_bits_y = count_y.bit_length() - 1
    levels_x = local_bits_x + device_bits_x
    levels_y = local_bits_y + device_bits_y
    place_x = lax.axis_index("gx")
    place_y = lax.axis_index("gy")
    quad_block = complex_block(quad.reshape(4, 4, 2, P_SIZE, P_SIZE))
    pair_block = complex_block(pair.reshape(2, 2, 2, P_SIZE, P_SIZE))
    center_x = ((place_x * boxes_x + jnp.arange(boxes_x)).astype(jnp.float32) + 0.5) / float(
        boxes_x * count_x
    ) - 0.5
    center_y = ((place_y * boxes_y + jnp.arange(boxes_y)).astype(jnp.float32) + 0.5) / float(
        boxes_y * count_y
    ) - 0.5
    angle = (
        slope[0][:, None, None] * center_x[None, :, None]
        + slope[1][:, None, None] * center_y[None, None, :]
    )
    cosine_table = jnp.cos(angle)
    sine_table = jnp.sin(angle)
    current = source.reshape(width_all, boxes_x, boxes_y)
    last_level = max(levels_x, levels_y)
    for depth in range(last_level):
        mode_x = "local" if depth < local_bits_x else "device" if depth < levels_x else "none"
        mode_y = "local" if depth < local_bits_y else "device"
        neighbours = {(0, 0): current}
        target_x = 0
        target_y = 0
        if mode_x == "device":
            shift_x = depth - local_bits_x
            shift_y = depth - local_bits_y
            target_x = place_x // (1 << shift_x) % 2
            target_y = place_y // (1 << shift_y) % 2
            across_x = partner(current, "gx", shift_x)
            paired = partner(jnp.stack([current, across_x]), "gy", shift_y)
            across_y = paired[0]
            across_both = paired[1]
            neighbours[1, 0] = across_x
            neighbours[0, 1] = across_y
            neighbours[1, 1] = across_both
        elif mode_y == "device":
            shift_y = depth - local_bits_y
            target_y = place_y // (1 << shift_y) % 2
            neighbours[0, 1] = partner(current, "gy", shift_y)
        merged = translate(
            neighbours, mode_x, mode_y, depth, target_x, target_y, quad_block, pair_block
        )
        current = rotate(merged, cosine_table, sine_table)
    return current.reshape(width_all, 1, 1, boxes_x * boxes_y)

LANES = 128
CHIPS = 16
BF16 = jnp.bfloat16
F32 = jnp.float32
MESH_ID = pl.DeviceIdType.MESH


def plan():
    slots = [("i", 4), ("i", 3), ("i", 2)]
    lanes = {64: ("i", 1), 32: ("i", 0)}
    for bit in range(5):
        lanes[1 << bit] = ("j", bit)
    steps = []
    for level in range(5):
        swaps = []
        need = [("i", level), ("j", level)]
        for bit in need:
            if bit in slots:
                continue
            stride = [s for s in lanes if lanes[s] == bit][0]
            free = [k for k in range(3) if slots[k] not in need]
            slot = free[0]
            swaps.append((slot, stride))
            slots[slot], lanes[stride] = lanes[stride], slots[slot]
        steps.append((swaps, slots.index(need[0]), slots.index(need[1])))
    return steps, slots, lanes


STEPS, END_SLOTS, END_LANES = plan()


def home_columns():
    columns = np.zeros(1024, np.int64)
    for place in range(1024):
        block, lane = place // LANES, place % LANES
        values = {END_SLOTS[k]: block >> (2 - k) & 1 for k in range(3)}
        for stride in END_LANES:
            values[END_LANES[stride]] = 1 if lane & stride else 0
        i = sum(values["i", b] << b for b in range(5))
        j = sum(values["j", b] << b for b in range(5))
        columns[place] = i * 32 + j
    return columns


def swap_pair(first, second, stride):
    mask = (lax.broadcasted_iota(jnp.int32, first.shape, 1) & stride) == 0
    low = jnp.where(mask, first, pltpu.roll(second, stride, 1))
    high = jnp.where(mask, pltpu.roll(first, LANES - stride, 1), second)
    return low, high


def slot_index(bits):
    return bits[0] * 4 + bits[1] * 2 + bits[2]


def turn(merged, cosine, sine):
    real_part, imag_part = merged[:P_SIZE], merged[P_SIZE:]
    return jnp.concatenate(
        [real_part * cosine - imag_part * sine, real_part * sine + imag_part * cosine], 0
    ).astype(BF16)


def assemble(matrix_ref, weight_ref, count):
    kept = count * 2 * LANES
    for t in range(count):
        parts = [
            [matrix_ref[(t * count + c) * 2 + r] for r in range(2)] for c in range(count)
        ]
        for out in range(2):
            rows = slice((t * 2 + out) * P_SIZE, (t * 2 + out + 1) * P_SIZE)
            rests = []
            for c in range(count):
                for side in range(2):
                    piece = parts[c][out ^ side]
                    if side == 1 and out == 0:
                        piece = -piece
                    first = (c * 2 + side) * LANES
                    weight_ref[rows, first : first + LANES] = piece[:, :LANES]
                    rests.append(piece[:, LANES:])
            weight_ref[rows, kept : kept + 16 * len(rests)] = jnp.concatenate(rests, 1)


def stack_children(children):
    mains = []
    rests = []
    for child in children:
        for side in range(2):
            first = side * P_SIZE
            mains.append(child[first : first + LANES])
            rests.append(child[first + LANES : first + P_SIZE])
    return jnp.concatenate(mains + rests, 0)


def near_kernel(source_ref, table_ref, matrix_ref, out_ref, table_out, weight_ref, state):
    width = 2 * P_SIZE
    assemble(matrix_ref, weight_ref, 4)
    for block in range(8):
        columns = pl.ds(block * LANES, LANES)
        state[block, 0:width, :] = source_ref[:, columns]
        state[block, width : 2 * width, :] = table_ref[:, columns]
    for swaps, slot_x, slot_y in STEPS:
        for slot, stride in swaps:
            mask = 4 >> slot
            for block in range(8):
                if not block & mask:
                    low, high = swap_pair(state[block], state[block | mask], stride)
                    state[block] = low
                    state[block | mask] = high
        rest = 3 - slot_x - slot_y

        def at(tx, ty, g):
            bits = [0, 0, 0]
            bits[slot_x], bits[slot_y], bits[rest] = tx, ty, g
            return slot_index(bits)

        stacked = stack_children(
            [
                jnp.concatenate([state[at(c // 2, c % 2, g), 0:width, :] for g in range(2)], 1)
                for c in range(4)
            ]
        )
        for t in range(4):
            merged = jnp.dot(
                weight_ref[t * width : (t + 1) * width, :], stacked, preferred_element_type=F32
            )
            for g in range(2):
                block = at(t // 2, t % 2, g)
                table = state[block, width : 2 * width, :].astype(F32)
                state[block, 0:width, :] = turn(
                    merged[:, g * LANES : (g + 1) * LANES], table[:P_SIZE], table[P_SIZE:]
                )
    for block in range(8):
        low, high = swap_pair(
            state[block, 0:P_SIZE, :], state[block, P_SIZE:width, :], 64
        )
        out_ref[2 * block] = low
        out_ref[2 * block + 1] = high
        table_out[block] = state[block, width : 2 * width, :]


def far_kernel(
    own_ref, table_ref, shift_ref, weight_ref, matrix_ref, out_ref, state, tables, other, pair_ref
):
    width = 2 * P_SIZE
    assemble(matrix_ref, pair_ref, 2)
    half = lax.axis_index("gy") // 2 % 2
    chip = lax.axis_index("gx") * 4 + lax.axis_index("gy") // 2
    core = lax.axis_index("gy") % 2
    lane = lax.broadcasted_iota(jnp.int32, (P_SIZE, LANES), 1)
    keep = (lane // 64) == half
    table = table_ref[chip // 2].astype(F32)
    base = []
    for k in range(2):
        part = table[k * P_SIZE : (k + 1) * P_SIZE]
        base.append(jnp.where(keep, part, pltpu.roll(part, 64, 1)))

    def chip_of(y, x, z1, z0):
        return y * 8 + x * 4 + z1 * 2 + z0

    for y in range(2):
        for x in range(2):
            for z0 in range(2):
                block = y * 4 + x * 2 + z0
                pick = []
                for k in range(2):
                    low = shift_ref[k, :, chip_of(y, x, 0, z0) : chip_of(y, x, 0, z0) + 1]
                    high = shift_ref[k, :, chip_of(y, x, 1, z0) : chip_of(y, x, 1, z0) + 1]
                    pick.append(jnp.where(lane < 64, low, high))
                tables[block, 0] = base[0] * pick[0] - base[1] * pick[1]
                tables[block, 1] = base[0] * pick[1] + base[1] * pick[0]
                for step in range(2):
                    low, high = swap_pair(
                        own_ref[step, chip_of(y, x, 0, z0)], own_ref[step, chip_of(y, x, 1, z0)], 64
                    )
                    target = state if step == 0 else other
                    target[block, 0:P_SIZE, :] = low
                    target[block, P_SIZE:width, :] = high

    def emit(merged, blocks):
        for n, block in enumerate(blocks):
            state[block] = turn(
                merged[:, n * LANES : (n + 1) * LANES], tables[block, 0], tables[block, 1]
            )

    groups = [(y, z0) for y in range(2) for z0 in range(2)]
    is_first = core == 0
    children = []
    for x in range(2):
        mine, theirs = [
            jnp.concatenate([ref[y * 4 + x * 2 + z0] for y, z0 in groups], 1)
            for ref in (state, other)
        ]
        children += [jnp.where(is_first, mine, theirs), jnp.where(is_first, theirs, mine)]
    stacked = stack_children(children)
    for x in range(2):
        row = pl.multiple_of((x * 2 + core) * width, width)
        merged = jnp.dot(
            weight_ref[pl.ds(row, width), :], stacked, preferred_element_type=F32
        )
        emit(merged, [y * 4 + x * 2 + z0 for y, z0 in groups])
    stacked = stack_children(
        [
            jnp.concatenate([state[c // 2 * 4 + x * 2 + c % 2] for x in range(2)], 1)
            for c in range(4)
        ]
    )
    for t in range(4):
        merged = jnp.dot(
            weight_ref[t * width : (t + 1) * width, :], stacked, preferred_element_type=F32
        )
        emit(merged, [t // 2 * 4 + x * 2 + t % 2 for x in range(2)])
    for block in range(4):
        low, high = swap_pair(state[block], state[block + 4], 64)
        state[block] = low
        state[block + 4] = high
        for k in range(2):
            low, high = swap_pair(tables[block, k], tables[block + 4, k], 64)
            tables[block, k] = low
            tables[block + 4, k] = high
    stacked = stack_children(
        [jnp.concatenate([state[c * 4 + g] for g in range(4)], 1) for c in range(2)]
    )
    for t in range(2):
        merged = jnp.dot(
            pair_ref[t * width : (t + 1) * width, :], stacked, preferred_element_type=F32
        )
        emit(merged, [t * 4 + g for g in range(4)])
    for z1 in range(2):
        for x in range(2):
            for z0 in range(2):
                block = z1 * 4 + x * 2 + z0
                low, high = swap_pair(
                    state[block, 0:P_SIZE, :], state[block, P_SIZE:width, :], 64
                )
                out_ref[chip_of(0, x, z1, z0)] = low
                out_ref[chip_of(1, x, z1, z0)] = high


def home_kernel(block_ref, order_ref, out_ref, state):
    for block in range(8):
        low, high = swap_pair(block_ref[2 * block], block_ref[2 * block + 1], 64)
        columns = slice(block * LANES, (block + 1) * LANES)
        state[0:P_SIZE, columns] = low
        state[P_SIZE : 2 * P_SIZE, columns] = high
    for part in range(4):
        columns = slice(part * 256, (part + 1) * 256)
        out_ref[:, columns] = jnp.dot(
            state[...], order_ref[:, columns], preferred_element_type=F32
        ).astype(BF16)


def trade_kernel(both, in_ref, out_ref, send_sem, recv_sem, pass_send, pass_recv, own_sem):
    gx = lax.axis_index("gx")
    gy = lax.axis_index("gy")
    core = gy % 2
    chip = gx * 4 + gy // 2
    mate = (gx, gy // 2 * 2 + (1 - core))

    def place(index):
        return (index // 4, index % 4 * 2 + core)

    barrier = pltpu.get_barrier_semaphore()
    for k in range(1, CHIPS):
        pl.semaphore_signal(
            barrier, inc=1, device_id=place((chip + k) % CHIPS), device_id_type=MESH_ID
        )
    if both:
        pl.semaphore_signal(barrier, inc=1, device_id=mate, device_id_type=MESH_ID)
    pl.semaphore_wait(barrier, CHIPS if both else CHIPS - 1)

    def landing(which, index):
        return out_ref.at[which, index] if both else out_ref.at[index]

    far_first = [(1, a, b) for a in range(4) for b in range(2)]
    far_first += [(0, a, b) for a in range(4) for b in range(2) if a or b]
    zed = gy // 2

    def across(hop, back):
        other_half, a, b = hop
        x = (gx + (4 - a if back else a)) % 4
        return x * 4 + (zed // 2 + other_half) % 2 * 2 + (zed + b) % 2

    sends = []
    for k in range(1, CHIPS):
        dest = across(far_first[k - 1], False)
        copy = pltpu.make_async_remote_copy(
            src_ref=in_ref.at[dest],
            dst_ref=landing(0, chip),
            send_sem=send_sem.at[k],
            recv_sem=recv_sem.at[k],
            device_id=place(dest),
            device_id_type=MESH_ID,
        )
        copy.start()
        sends.append(copy)
    own = pltpu.make_async_copy(in_ref.at[chip], landing(0, chip), own_sem)
    own.start()

    def forward(k, src):
        index = across(far_first[k - 1], True) if k else chip
        copy = pltpu.make_async_remote_copy(
            src_ref=src,
            dst_ref=landing(1, index),
            send_sem=pass_send.at[k],
            recv_sem=pass_recv.at[k],
            device_id=mate,
            device_id_type=MESH_ID,
        )
        copy.start()
        return copy

    passes = []
    if both:
        passes.append(forward(0, in_ref.at[chip]))
    for k in range(1, CHIPS):
        sends[k - 1].wait_recv()
        if both:
            passes.append(forward(k, landing(0, across(far_first[k - 1], True))))
    own.wait()
    for copy in sends:
        copy.wait_send()
    for copy in passes:
        copy.wait()


def trade(blocks, both, identity):
    shape = ((2,) if both else ()) + blocks.shape
    return pl.pallas_call(
        functools.partial(trade_kernel, both),
        out_shape=jax.ShapeDtypeStruct(shape, BF16),
        in_specs=[pl.BlockSpec(memory_space=pl.ANY)],
        out_specs=pl.BlockSpec(memory_space=pl.ANY),
        scratch_shapes=[pltpu.SemaphoreType.DMA((CHIPS,))] * 4 + [pltpu.SemaphoreType.DMA],
        compiler_params=pltpu.CompilerParams(collective_id=identity, has_side_effects=True),
    )(blocks)


def turned(angle):
    return jnp.cos(angle), jnp.sin(angle)


def traded(source, slope, quad, pair):
    width_all = source.shape[0]
    count_x = lax.axis_size("gx")
    count_y = lax.axis_size("gy")
    place_x = lax.axis_index("gx")
    place_y = lax.axis_index("gy")
    core = place_y % 2
    total_x = float(SIDE * count_x)
    total_y = float(SIDE * count_y)
    steps = jnp.arange(SIDE)
    center_x = ((place_x * SIDE + steps).astype(F32) + 0.5) / total_x - 0.5
    center_y = ((place_y * SIDE + steps).astype(F32) + 0.5) / total_y - 0.5
    tiles = jnp.arange(CHIPS)
    far_x = ((tiles // 4 - place_x) * SIDE).astype(F32) / total_x
    far_y = ((tiles % 4 * 2 + core - place_y) * SIDE).astype(F32) / total_y
    angle = jnp.concatenate(
        [
            slope[0][:, None] * center_x[None],
            slope[1][:, None] * center_y[None],
            slope[0][:, None] * far_x[None] + slope[1][:, None] * far_y[None],
        ],
        1,
    )
    cosine, sine = turned(angle)
    cos_x, sin_x = cosine[:, :SIDE, None], sine[:, :SIDE, None]
    cos_y, sin_y = cosine[:, None, SIDE : 2 * SIDE], sine[:, None, SIDE : 2 * SIDE]
    table = jnp.concatenate([cos_x * cos_y - sin_x * sin_y, cos_x * sin_y + sin_x * cos_y], 0)
    table = table.astype(BF16).reshape(width_all, SIDE * SIDE)
    shift = jnp.stack([cosine[:, 2 * SIDE :], sine[:, 2 * SIDE :]])
    matrices = quad.reshape(32, P_SIZE, P_SIZE)
    pairs = pair.reshape(8, P_SIZE, P_SIZE)
    order = jnp.asarray(home_columns()[:, None] == np.arange(SIDE * SIDE)[None], BF16)
    roomy = pltpu.CompilerParams(vmem_limit_bytes=50 * 1024 * 1024)
    block_shape = jax.ShapeDtypeStruct((CHIPS, P_SIZE, LANES), BF16)
    blocks, near_table, weight = pl.pallas_call(
        near_kernel,
        out_shape=(
            block_shape,
            jax.ShapeDtypeStruct((8, width_all, LANES), BF16),
            jax.ShapeDtypeStruct((4 * width_all, 4 * width_all), BF16),
        ),
        scratch_shapes=[pltpu.VMEM((8, 2 * width_all, LANES), BF16)],
        compiler_params=roomy,
    )(source.reshape(width_all, SIDE * SIDE), table, matrices)
    gathered = trade(blocks, True, 0)
    results = pl.pallas_call(
        far_kernel,
        out_shape=block_shape,
        scratch_shapes=[
            pltpu.VMEM((8, width_all, LANES), BF16),
            pltpu.VMEM((8, 2, P_SIZE, LANES), F32),
            pltpu.VMEM((8, width_all, LANES), BF16),
            pltpu.VMEM((2 * width_all, 2 * width_all), BF16),
        ],
        compiler_params=roomy,
    )(gathered, near_table, shift, weight, pairs)
    returned = trade(results, False, 1)
    image = pl.pallas_call(
        home_kernel,
        out_shape=jax.ShapeDtypeStruct((width_all, SIDE * SIDE), BF16),
        scratch_shapes=[pltpu.VMEM((width_all, SIDE * SIDE), BF16)],
        compiler_params=roomy,
    )(returned, order)
    return image.reshape(width_all, 1, 1, SIDE * SIDE)


def solution(mesh):
    in_specs = (P(None, "gx", "gy", None), P(), P(), P())
    out_specs = P(None, "gx", "gy", None)
    fits = mesh.shape["gx"] == 4 and mesh.shape["gy"] == 8
    body = traded if fits else local
    return jax.shard_map(body, mesh=mesh, in_specs=in_specs, out_specs=out_specs, check_vma=False)
```

```python
import functools
import jax
import jax.numpy as jnp
import numpy as np
from jax import lax
from jax.experimental import pallas as pl
from jax.experimental.pallas import tpu as pltpu
from jax.sharding import PartitionSpec as P

P_SIZE = 144
SIDE = 32


def partner(value, axis, stride):
    mask = 2**stride
    pairs = [(source, source ^ mask) for source in range(lax.axis_size(axis))]
    return lax.ppermute(value, axis, pairs)


def complex_block(coefficients):
    real_part = coefficients[..., 0, :, :]
    imag_part = coefficients[..., 1, :, :]
    upper_rows = jnp.concatenate([real_part, -imag_part], -1)
    lower_rows = jnp.concatenate([imag_part, real_part], -1)
    return jnp.concatenate([upper_rows, lower_rows], -2)


def translate(neighbours, mode_x, mode_y, depth, target_x, target_y, quad_block, pair_block):
    width_all, boxes_x, boxes_y = neighbours[0, 0].shape
    split_x = 2 if mode_x == "local" else 1
    inner_x = 1 << depth if mode_x == "local" else 1
    split_y = 2 if mode_y == "local" else 1
    inner_y = 1 << depth if mode_y == "local" else 1
    shape_seven = (
        width_all,
        boxes_x // (split_x * inner_x),
        split_x,
        inner_x,
        boxes_y // (split_y * inner_y),
        split_y,
        inner_y,
    )
    shaped = {}
    for source_key in neighbours:
        shaped[source_key] = neighbours[source_key].reshape(shape_seven)
    steps_x = [0, 1] if mode_x != "none" else [0]
    steps_y = [0, 1]
    stacked_rows = []
    for slot_x in range(split_x):
        columns = []
        for slot_y in range(split_y):
            chosen_x = slot_x if mode_x == "local" else target_x
            chosen_y = slot_y if mode_y == "local" else target_y
            summed = None
            for step_x in steps_x:
                for step_y in steps_y:
                    source_key = (
                        step_x if mode_x == "device" else 0,
                        step_y if mode_y == "device" else 0,
                    )
                    from_x = (slot_x + step_x) % 2 if mode_x == "local" else 0
                    from_y = (slot_y + step_y) % 2 if mode_y == "local" else 0
                    block_rows = shaped[source_key][:, :, from_x, :, :, from_y, :]
                    child_x = (chosen_x + step_x) % 2
                    child_y = (chosen_y + step_y) % 2
                    if mode_x == "none":
                        matrix = pair_block[chosen_y, child_y]
                    else:
                        matrix = quad_block[chosen_x * 2 + chosen_y, child_x * 2 + child_y]
                    product_term = jnp.dot(
                        matrix,
                        block_rows.reshape(width_all, -1),
                        preferred_element_type=jnp.float32,
                    )
                    summed = product_term if summed is None else summed + product_term
            columns.append(summed.reshape(block_rows.shape))
        stacked_rows.append(jnp.stack(columns, 4))
    return jnp.stack(stacked_rows, 2).reshape(width_all, boxes_x, boxes_y)


def rotate(merged, cosine_table, sine_table):
    half_width = merged.shape[0] // 2
    real_part = merged[:half_width]
    imag_part = merged[half_width:]
    return jnp.concatenate(
        [
            real_part * cosine_table - imag_part * sine_table,
            real_part * sine_table + imag_part * cosine_table,
        ],
        0,
    ).astype(jnp.bfloat16)


def local(source, slope, quad, pair):
    width_all = source.shape[0]
    boxes_x = SIDE
    boxes_y = SIDE
    count_x = lax.axis_size("gx")
    count_y = lax.axis_size("gy")
    local_bits_x = boxes_x.bit_length() - 1
    local_bits_y = boxes_y.bit_length() - 1
    device_bits_x = count_x.bit_length() - 1
    device_bits_y = count_y.bit_length() - 1
    levels_x = local_bits_x + device_bits_x
    levels_y = local_bits_y + device_bits_y
    place_x = lax.axis_index("gx")
    place_y = lax.axis_index("gy")
    quad_block = complex_block(quad.reshape(4, 4, 2, P_SIZE, P_SIZE))
    pair_block = complex_block(pair.reshape(2, 2, 2, P_SIZE, P_SIZE))
    center_x = ((place_x * boxes_x + jnp.arange(boxes_x)).astype(jnp.float32) + 0.5) / float(
        boxes_x * count_x
    ) - 0.5
    center_y = ((place_y * boxes_y + jnp.arange(boxes_y)).astype(jnp.float32) + 0.5) / float(
        boxes_y * count_y
    ) - 0.5
    angle = (
        slope[0][:, None, None] * center_x[None, :, None]
        + slope[1][:, None, None] * center_y[None, None, :]
    )
    cosine_table = jnp.cos(angle)
    sine_table = jnp.sin(angle)
    current = source.reshape(width_all, boxes_x, boxes_y)
    last_level = max(levels_x, levels_y)
    for depth in range(last_level):
        mode_x = "local" if depth < local_bits_x else "device" if depth < levels_x else "none"
        mode_y = "local" if depth < local_bits_y else "device"
        neighbours = {(0, 0): current}
        target_x = 0
        target_y = 0
        if mode_x == "device":
            shift_x = depth - local_bits_x
            shift_y = depth - local_bits_y
            target_x = place_x // (1 << shift_x) % 2
            target_y = place_y // (1 << shift_y) % 2
            across_x = partner(current, "gx", shift_x)
            paired = partner(jnp.stack([current, across_x]), "gy", shift_y)
            across_y = paired[0]
            across_both = paired[1]
            neighbours[1, 0] = across_x
            neighbours[0, 1] = across_y
            neighbours[1, 1] = across_both
        elif mode_y == "device":
            shift_y = depth - local_bits_y
            target_y = place_y // (1 << shift_y) % 2
            neighbours[0, 1] = partner(current, "gy", shift_y)
        merged = translate(
            neighbours, mode_x, mode_y, depth, target_x, target_y, quad_block, pair_block
        )
        current = rotate(merged, cosine_table, sine_table)
    return current.reshape(width_all, 1, 1, boxes_x * boxes_y)

LANES = 128
CHIPS = 16
BF16 = jnp.bfloat16
F32 = jnp.float32
MESH_ID = pl.DeviceIdType.MESH


def plan():
    slots = [("i", 4), ("i", 3), ("i", 2)]
    lanes = {64: ("i", 1), 32: ("i", 0)}
    for bit in range(5):
        lanes[1 << bit] = ("j", bit)
    steps = []
    for level in range(5):
        swaps = []
        need = [("i", level), ("j", level)]
        for bit in need:
            if bit in slots:
                continue
            stride = [s for s in lanes if lanes[s] == bit][0]
            free = [k for k in range(3) if slots[k] not in need]
            slot = free[0]
            swaps.append((slot, stride))
            slots[slot], lanes[stride] = lanes[stride], slots[slot]
        steps.append((swaps, slots.index(need[0]), slots.index(need[1])))
    return steps, slots, lanes


STEPS, END_SLOTS, END_LANES = plan()


def home_columns():
    columns = np.zeros(1024, np.int64)
    for place in range(1024):
        block, lane = place // LANES, place % LANES
        values = {END_SLOTS[k]: block >> (2 - k) & 1 for k in range(3)}
        for stride in END_LANES:
            values[END_LANES[stride]] = 1 if lane & stride else 0
        i = sum(values["i", b] << b for b in range(5))
        j = sum(values["j", b] << b for b in range(5))
        columns[place] = i * 32 + j
    return columns


def swap_pair(first, second, stride):
    mask = (lax.broadcasted_iota(jnp.int32, first.shape, 1) & stride) == 0
    low = jnp.where(mask, first, pltpu.roll(second, stride, 1))
    high = jnp.where(mask, pltpu.roll(first, LANES - stride, 1), second)
    return low, high


def slot_index(bits):
    return bits[0] * 4 + bits[1] * 2 + bits[2]


def turn(merged, cosine, sine):
    real_part, imag_part = merged[:P_SIZE], merged[P_SIZE:]
    return jnp.concatenate(
        [real_part * cosine - imag_part * sine, real_part * sine + imag_part * cosine], 0
    ).astype(BF16)


def assemble(matrix_ref, weight_ref, count):
    kept = count * 2 * LANES
    for t in range(count):
        parts = [
            [matrix_ref[(t * count + c) * 2 + r] for r in range(2)] for c in range(count)
        ]
        for out in range(2):
            rows = slice((t * 2 + out) * P_SIZE, (t * 2 + out + 1) * P_SIZE)
            rests = []
            for c in range(count):
                for side in range(2):
                    piece = parts[c][out ^ side]
                    if side == 1 and out == 0:
                        piece = -piece
                    first = (c * 2 + side) * LANES
                    weight_ref[rows, first : first + LANES] = piece[:, :LANES]
                    rests.append(piece[:, LANES:])
            weight_ref[rows, kept : kept + 16 * len(rests)] = jnp.concatenate(rests, 1)


def stack_children(children):
    mains = []
    rests = []
    for child in children:
        for side in range(2):
            first = side * P_SIZE
            mains.append(child[first : first + LANES])
            rests.append(child[first + LANES : first + P_SIZE])
    return jnp.concatenate(mains + rests, 0)


def near_kernel(source_ref, table_ref, matrix_ref, out_ref, table_out, weight_ref, state):
    width = 2 * P_SIZE
    assemble(matrix_ref, weight_ref, 4)
    for block in range(8):
        columns = pl.ds(block * LANES, LANES)
        state[block, 0:width, :] = source_ref[:, columns]
        state[block, width : 2 * width, :] = table_ref[:, columns]
    for swaps, slot_x, slot_y in STEPS:
        for slot, stride in swaps:
            mask = 4 >> slot
            for block in range(8):
                if not block & mask:
                    low, high = swap_pair(state[block], state[block | mask], stride)
                    state[block] = low
                    state[block | mask] = high
        rest = 3 - slot_x - slot_y

        def at(tx, ty, g):
            bits = [0, 0, 0]
            bits[slot_x], bits[slot_y], bits[rest] = tx, ty, g
            return slot_index(bits)

        stacked = stack_children(
            [
                jnp.concatenate([state[at(c // 2, c % 2, g), 0:width, :] for g in range(2)], 1)
                for c in range(4)
            ]
        )
        for t in range(4):
            merged = jnp.dot(
                weight_ref[t * width : (t + 1) * width, :], stacked, preferred_element_type=F32
            )
            for g in range(2):
                block = at(t // 2, t % 2, g)
                table = state[block, width : 2 * width, :].astype(F32)
                state[block, 0:width, :] = turn(
                    merged[:, g * LANES : (g + 1) * LANES], table[:P_SIZE], table[P_SIZE:]
                )
    for block in range(8):
        low, high = swap_pair(
            state[block, 0:P_SIZE, :], state[block, P_SIZE:width, :], 64
        )
        out_ref[2 * block] = low
        out_ref[2 * block + 1] = high
        table_out[block] = state[block, width : 2 * width, :]


def chip_of(y, x, z1, z0):
    return y * 8 + x * 4 + z1 * 2 + z0


def far_tables(table_ref, shift_ref, tables):
    half = lax.axis_index("gy") // 2 % 2
    chip = lax.axis_index("gx") * 4 + lax.axis_index("gy") // 2
    lane = lax.broadcasted_iota(jnp.int32, (P_SIZE, LANES), 1)
    keep = (lane // 64) == half
    table = table_ref[chip // 2].astype(F32)
    base = []
    for k in range(2):
        part = table[k * P_SIZE : (k + 1) * P_SIZE]
        base.append(jnp.where(keep, part, pltpu.roll(part, 64, 1)))
    for y in range(2):
        for x in range(2):
            for z0 in range(2):
                block = y * 4 + x * 2 + z0
                pick = []
                for k in range(2):
                    low = shift_ref[k, :, chip_of(y, x, 0, z0) : chip_of(y, x, 0, z0) + 1]
                    high = shift_ref[k, :, chip_of(y, x, 1, z0) : chip_of(y, x, 1, z0) + 1]
                    pick.append(jnp.where(lane < 64, low, high))
                tables[block, 0] = base[0] * pick[0] - base[1] * pick[1]
                tables[block, 1] = base[0] * pick[1] + base[1] * pick[0]


def far_kernel(own_ref, weight_ref, pair_ref, out_ref, state, tables, other):
    width = 2 * P_SIZE
    core = lax.axis_index("gy") % 2
    for y in range(2):
        for x in range(2):
            for z0 in range(2):
                block = y * 4 + x * 2 + z0
                for step in range(2):
                    low, high = swap_pair(
                        own_ref[step, chip_of(y, x, 0, z0)], own_ref[step, chip_of(y, x, 1, z0)], 64
                    )
                    target = state if step == 0 else other
                    target[block, 0:P_SIZE, :] = low
                    target[block, P_SIZE:width, :] = high

    def emit(merged, blocks):
        for n, block in enumerate(blocks):
            state[block] = turn(
                merged[:, n * LANES : (n + 1) * LANES], tables[block, 0], tables[block, 1]
            )

    groups = [(y, z0) for y in range(2) for z0 in range(2)]
    is_first = core == 0
    children = []
    for x in range(2):
        mine, theirs = [
            jnp.concatenate([ref[y * 4 + x * 2 + z0] for y, z0 in groups], 1)
            for ref in (state, other)
        ]
        children += [jnp.where(is_first, mine, theirs), jnp.where(is_first, theirs, mine)]
    stacked = stack_children(children)
    for x in range(2):
        row = pl.multiple_of((x * 2 + core) * width, width)
        merged = jnp.dot(
            weight_ref[pl.ds(row, width), :], stacked, preferred_element_type=F32
        )
        emit(merged, [y * 4 + x * 2 + z0 for y, z0 in groups])
    stacked = stack_children(
        [
            jnp.concatenate([state[c // 2 * 4 + x * 2 + c % 2] for x in range(2)], 1)
            for c in range(4)
        ]
    )
    for t in range(4):
        merged = jnp.dot(
            weight_ref[t * width : (t + 1) * width, :], stacked, preferred_element_type=F32
        )
        emit(merged, [t // 2 * 4 + x * 2 + t % 2 for x in range(2)])
    for block in range(4):
        low, high = swap_pair(state[block], state[block + 4], 64)
        state[block] = low
        state[block + 4] = high
        for k in range(2):
            low, high = swap_pair(tables[block, k], tables[block + 4, k], 64)
            tables[block, k] = low
            tables[block + 4, k] = high
    stacked = stack_children(
        [jnp.concatenate([state[c * 4 + g] for g in range(4)], 1) for c in range(2)]
    )
    for t in range(2):
        merged = jnp.dot(
            pair_ref[t * width : (t + 1) * width, :], stacked, preferred_element_type=F32
        )
        emit(merged, [t * 4 + g for g in range(4)])
    for z1 in range(2):
        for x in range(2):
            for z0 in range(2):
                block = z1 * 4 + x * 2 + z0
                low, high = swap_pair(
                    state[block, 0:P_SIZE, :], state[block, P_SIZE:width, :], 64
                )
                out_ref[chip_of(0, x, z1, z0)] = low
                out_ref[chip_of(1, x, z1, z0)] = high


def home_kernel(block_ref, order_ref, out_ref, state):
    for block in range(8):
        low, high = swap_pair(block_ref[2 * block], block_ref[2 * block + 1], 64)
        columns = slice(block * LANES, (block + 1) * LANES)
        state[0:P_SIZE, columns] = low
        state[P_SIZE : 2 * P_SIZE, columns] = high
    for part in range(4):
        columns = slice(part * 256, (part + 1) * 256)
        out_ref[:, columns] = jnp.dot(
            state[...], order_ref[:, columns], preferred_element_type=F32
        ).astype(BF16)


def whole_kernel(
    source_ref,
    table_ref,
    matrix_ref,
    shift_ref,
    pairs_ref,
    order_hbm,
    image_ref,
    blocks,
    near_table,
    weight,
    near_state,
    gathered,
    state,
    tables,
    other,
    pair_weight,
    results,
    returned,
    home,
    order,
    send_sem,
    recv_sem,
    pass_send,
    pass_recv,
    back_send,
    back_recv,
    own_sem,
):
    gx = lax.axis_index("gx")
    gy = lax.axis_index("gy")
    core = gy % 2
    zed = gy // 2
    chip = gx * 4 + zed
    mate = (gx, zed * 2 + (1 - core))
    hops = [(1, a, b) for a in range(4) for b in range(2)]
    hops += [(0, a, b) for a in range(4) for b in range(2) if a or b]

    def place(index):
        return (index // 4, index % 4 * 2 + core)

    def across(hop, back):
        other_half, a, b = hop
        x = (gx + (4 - a if back else a)) % 4
        return x * 4 + (zed // 2 + other_half) % 2 * 2 + (zed + b) % 2

    barrier = pltpu.get_barrier_semaphore()
    for hop in hops:
        pl.semaphore_signal(
            barrier, inc=1, device_id=place(across(hop, False)), device_id_type=MESH_ID
        )
    pl.semaphore_signal(barrier, inc=1, device_id=mate, device_id_type=MESH_ID)
    order_copy = pltpu.make_async_copy(order_hbm, order, own_sem.at[2])
    order_copy.start()
    near_kernel(source_ref, table_ref, matrix_ref, blocks, near_table, weight, near_state)
    pl.semaphore_wait(barrier, CHIPS)

    def post(source, landing, send, recv):
        copies = []
        for k, hop in enumerate(hops):
            dest = across(hop, False)
            copy = pltpu.make_async_remote_copy(
                src_ref=source.at[dest],
                dst_ref=landing.at[chip],
                send_sem=send.at[k],
                recv_sem=recv.at[k],
                device_id=place(dest),
                device_id_type=MESH_ID,
            )
            copy.start()
            copies.append(copy)
        return copies

    def forward(k, src, index):
        copy = pltpu.make_async_remote_copy(
            src_ref=src,
            dst_ref=gathered.at[1, index],
            send_sem=pass_send.at[k],
            recv_sem=pass_recv.at[k],
            device_id=mate,
            device_id_type=MESH_ID,
        )
        copy.start()
        return copy

    sends = post(blocks, gathered.at[0], send_sem, recv_sem)
    own = pltpu.make_async_copy(blocks.at[chip], gathered.at[0, chip], own_sem.at[0])
    own.start()
    passes = [forward(15, blocks.at[chip], chip)]
    assemble(pairs_ref, pair_weight, 2)
    far_tables(near_table, shift_ref, tables)
    for k, hop in enumerate(hops):
        sends[k].wait_recv()
        index = across(hop, True)
        passes.append(forward(k, gathered.at[0, index], index))
    own.wait()
    for copy in passes:
        copy.wait()
    far_kernel(gathered, weight, pair_weight, results, state, tables, other)
    backs = post(results, returned, back_send, back_recv)
    own = pltpu.make_async_copy(results.at[chip], returned.at[chip], own_sem.at[1])
    own.start()
    order_copy.wait()
    own.wait()
    for copy in sends:
        copy.wait_send()
    for copy in backs:
        copy.wait()
    home_kernel(returned, order, image_ref, home)


def turned(angle):
    return jnp.cos(angle), jnp.sin(angle)


def traded(source, slope, quad, pair):
    width_all = source.shape[0]
    count_x = lax.axis_size("gx")
    count_y = lax.axis_size("gy")
    place_x = lax.axis_index("gx")
    place_y = lax.axis_index("gy")
    core = place_y % 2
    total_x = float(SIDE * count_x)
    total_y = float(SIDE * count_y)
    steps = jnp.arange(SIDE)
    center_x = ((place_x * SIDE + steps).astype(F32) + 0.5) / total_x - 0.5
    center_y = ((place_y * SIDE + steps).astype(F32) + 0.5) / total_y - 0.5
    tiles = jnp.arange(CHIPS)
    far_x = ((tiles // 4 - place_x) * SIDE).astype(F32) / total_x
    far_y = ((tiles % 4 * 2 + core - place_y) * SIDE).astype(F32) / total_y
    angle = jnp.concatenate(
        [
            slope[0][:, None] * center_x[None],
            slope[1][:, None] * center_y[None],
            slope[0][:, None] * far_x[None] + slope[1][:, None] * far_y[None],
        ],
        1,
    )
    cosine, sine = turned(angle)
    cos_x, sin_x = cosine[:, :SIDE, None], sine[:, :SIDE, None]
    cos_y, sin_y = cosine[:, None, SIDE : 2 * SIDE], sine[:, None, SIDE : 2 * SIDE]
    table = jnp.concatenate([cos_x * cos_y - sin_x * sin_y, cos_x * sin_y + sin_x * cos_y], 0)
    table = table.astype(BF16).reshape(width_all, SIDE * SIDE)
    shift = jnp.stack([cosine[:, 2 * SIDE :], sine[:, 2 * SIDE :]])
    matrices = quad.reshape(32, P_SIZE, P_SIZE)
    pairs = pair.reshape(8, P_SIZE, P_SIZE)
    order = jnp.asarray(home_columns()[:, None] == np.arange(SIDE * SIDE)[None], BF16)
    vmem = pl.BlockSpec(memory_space=pltpu.VMEM)
    tile = (P_SIZE, LANES)
    size = SIDE * SIDE
    dma = pltpu.SemaphoreType.DMA
    image = pl.pallas_call(
        whole_kernel,
        out_shape=jax.ShapeDtypeStruct((width_all, size), BF16),
        in_specs=[vmem] * 5 + [pl.BlockSpec(memory_space=pl.ANY)],
        out_specs=vmem,
        scratch_shapes=[
            pltpu.VMEM((CHIPS,) + tile, BF16),
            pltpu.VMEM((8, width_all, LANES), BF16),
            pltpu.VMEM((4 * width_all, 4 * width_all), BF16),
            pltpu.VMEM((8, 2 * width_all, LANES), BF16),
            pltpu.VMEM((2, CHIPS) + tile, BF16),
            pltpu.VMEM((8, width_all, LANES), BF16),
            pltpu.VMEM((8, 2) + tile, F32),
            pltpu.VMEM((8, width_all, LANES), BF16),
            pltpu.VMEM((2 * width_all, 2 * width_all), BF16),
            pltpu.VMEM((CHIPS,) + tile, BF16),
            pltpu.VMEM((CHIPS,) + tile, BF16),
            pltpu.VMEM((width_all, size), BF16),
            pltpu.VMEM((size, size), BF16),
        ]
        + [dma((CHIPS,))] * 6
        + [dma((3,))],
        compiler_params=pltpu.CompilerParams(
            collective_id=0, has_side_effects=True, vmem_limit_bytes=50 * 1024 * 1024
        ),
    )(source.reshape(width_all, size), table, matrices, shift, pairs, order)
    return image.reshape(width_all, 1, 1, SIDE * SIDE)


def solution(mesh):
    in_specs = (P(None, "gx", "gy", None), P(), P(), P())
    out_specs = P(None, "gx", "gy", None)
    fits = mesh.shape["gx"] == 4 and mesh.shape["gy"] == 8
    body = traded if fits else local
    return jax.shard_map(body, mesh=mesh, in_specs=in_specs, out_specs=out_specs, check_vma=False)
```
